256 devices in a mesh: grp: 8 (over y, x_hi), pair: 32 (over x_lo, z, core).
Axes of the slice: x: 4 (x_hi: 2, x_lo: 2; x = x_hi * 2 + x_lo), y: 4, z: 8, core: 2. Of those that a mesh axis runs over, the one named last changes fastest.
Arguments:
- amplitudes: bfloat16 [96, 96, 9216], P('pair'), may hold values from -6 to 6
- integrals: bfloat16 [9216, 9216], P('pair', 'grp'), may hold values from -0.0625 to 0.0625
- live_counts: int32 [2], replicated, may hold values from 48 to 96, as said below
Outputs:
- residual: bfloat16 [96, 96, 9216], P('pair', None, 'grp')
The draws below stay inside these ranges and needn't reach their ends.
Inputs may be any that keep to these rules, and one draw needn't show every extreme that they name: `live_counts`: orbital slots at or beyond a count are padding; exactly one of the two counts equals 96.
All inputs are finite; a program needn't handle non-finite values.
Results may differ from the reference program's by a relative error of at most 0.001.
Values may be sent and summed in bfloat16 or wider, within the bound.
No kernel may reach another device: no remote copies, remote signals or barrier semaphores. Data moves between devices by JAX's collectives and lax.ppermute only.
A program may use at most 128 MiB of HBM per device.

```python
import jax
import jax.numpy as jnp

VB = 96
NOCC = 96
AB = 9216


def draw_live_counts(key, part):
    key = jax.random.fold_in(key, 7)
    first, second = jax.random.split(key)
    counts = jax.random.randint(first, (2,), VB // 2, VB)
    chosen = jax.random.randint(second, (), 0, 2)
    return jnp.where(jnp.arange(2) == chosen, VB, counts).astype(jnp.int32)


def level_of(key, shape, cuts, low, top_value):
    loudness, own = 1.0, jax.random.fold_in(key, 6)
    for axis_at, blocks in cuts:
        heights = jnp.exp(jax.random.uniform(jax.random.fold_in(own, axis_at), (blocks,), jnp.float32, low / len(cuts), top_value / len(cuts)))
        loudness = loudness * jnp.repeat(heights, shape[axis_at] // blocks).reshape([-1 if axis == axis_at else 1 for axis in range(len(shape))])
    return loudness


def scatter_about(rng, dims, spread, most, shards=(), held_as=jnp.bfloat16):
    drawn = jax.random.normal(rng, dims, jnp.float32) * spread
    if len(shards) > 0:
        drawn = level_of(rng, dims, shards, -0.22, 0.18) * drawn
    return jnp.clip(drawn, min=-most, max=most).astype(held_as)


def setup_inputs(seed: int = 0) -> dict:
    splits = jax.random.split(jax.random.key(seed), 4)
    return {
        "amplitudes": scatter_about(splits[0], (NOCC, NOCC, AB), 1.0, 6.0, ((0, 32),)),
        "integrals": scatter_about(splits[1], (AB, AB), AB ** -0.5, 0.0625, ((0, 32), (1, 8))),
        "live_counts": draw_live_counts(jax.random.fold_in(splits[3], 71), 0),
    }


def reference(amplitudes, integrals, live_counts):
    position = jnp.arange(VB * VB)
    keep_pairs = ((position // VB < live_counts[1]) & (position % VB < live_counts[1])).astype(jnp.bfloat16)
    flat_rows = (amplitudes * keep_pairs).reshape(NOCC * NOCC, VB * VB)
    ladder = jnp.dot(flat_rows, integrals, preferred_element_type=jnp.float32)
    ladder = ladder.reshape(NOCC, NOCC, VB, VB)
    summed = ladder + jnp.transpose(ladder, (1, 0, 3, 2))
    virtual = jnp.arange(VB)
    keep_out = ((virtual[:, None] < live_counts[0]) & (virtual[None, :] < live_counts[0])).astype(jnp.float32)
    return (summed * keep_out).reshape(NOCC, NOCC, VB * VB).astype(jnp.bfloat16)
```

```python
import jax
import jax.numpy as jnp
from jax import lax
from jax.sharding import Mesh
from jax.sharding import PartitionSpec as P

VB = 96
WIRE = jnp.float16
SCALE = 16.0


def on_device(amplitudes, integrals, live_counts):
    occ, nocc, k_all = amplitudes.shape
    shard, slab = integrals.shape
    rows, half, k_half = occ * nocc, slab // 2, k_all // 2
    xl = lax.axis_index("xl")
    pair = (xl * 8 + lax.axis_index("z")) * 2 + lax.axis_index("c")
    grp = lax.axis_index("y") * 2 + lax.axis_index("xh")
    swap = [(0, 1), (1, 0)]

    at = pair * shard + jnp.arange(shard)
    live = (at // VB < live_counts[1]) & (at % VB < live_counts[1])
    w = jnp.where(live[:, None], integrals, 0)
    w_keep = jnp.where(xl == 0, w[:, :half], w[:, half:])
    w_send = jnp.where(xl == 0, w[:, half:], w[:, :half])
    w_recv = lax.ppermute(w_send, "xl", swap)
    w_own = lax.all_gather(w_keep, ("z", "c"), axis=0, tiled=True)
    w_far = lax.all_gather(w_recv, ("z", "c"), axis=0, tiled=True)

    t = amplitudes.reshape(rows, k_all)
    t_own = lax.dynamic_slice(t, (0, xl * k_half), (rows, k_half))
    t_far = lax.dynamic_slice(t, (0, (1 - xl) * k_half), (rows, k_half))
    u_far = lax.ppermute(t_own, ("xh", "xl"), [(i, (i + 1) % 4) for i in range(4)])
    u_own = lax.ppermute(t_far, ("xh", "xl"), [(i, (i - 1) % 4) for i in range(4)])

    def dot(x, y):
        return jnp.dot(x, y, preferred_element_type=jnp.float32)

    mine = dot(t_own, w_own) + dot(t_far, w_far)
    other = dot(u_own, w_own) + dot(u_far, w_far)

    fetched = lax.ppermute(other, "xl", swap)
    low = jnp.where(xl == 0, mine, fetched)
    high = jnp.where(xl == 0, fetched, mine)
    direct = jnp.concatenate([low, high], axis=1)

    both = jnp.stack([jnp.where(xl == 0, mine, other), jnp.where(xl == 0, other, mine)])
    wire = (both * SCALE).astype(WIRE)
    wire = wire.reshape(2, occ, 32, 3, 6, 8, 12).transpose(2, 5, 3, 0, 1, 6, 4)
    got = lax.all_to_all(
        wire.reshape(256, -1), ("xl", "z", "c", "y", "xh"), 0, 0, tiled=True
    )
    got = got.reshape(2, 16, 8, 3, 2, 3, 12, 6)
    mirrored = got.transpose(3, 4, 1, 5, 6, 2, 0, 7).reshape(rows, slab)
    summed = direct + mirrored.astype(jnp.float32) * (1 / SCALE)

    col = jnp.arange(slab)
    keep = (grp * (slab // VB) + col // VB < live_counts[0]) & (col % VB < live_counts[0])
    return jnp.where(keep, summed, 0).reshape(occ, nocc, slab).astype(jnp.bfloat16)


def solution(mesh):
    fine = Mesh(mesh.devices.reshape(4, 2, 2, 8, 2), ("y", "xh", "xl", "z", "c"))
    pair, grp = ("xl", "z", "c"), ("y", "xh")
    return jax.shard_map(
        on_device,
        mesh=fine,
        in_specs=(P(pair, None, None), P(pair, grp), P()),
        out_specs=P(pair, None, grp),
        check_vma=False,
    )
```

```python
import functools

import jax
import jax.numpy as jnp
from jax import lax
from jax.experimental import pallas as pl
from jax.experimental.pallas import tpu as pltpu
from jax.sharding import Mesh
from jax.sharding import PartitionSpec as P

VB = 96
OCC = 3
GRPS = 8
PAIRS = 32
SLAB = VB // GRPS
TILE = SLAB * SLAB
WIRE = jnp.float16
SCALE = 16.0
BF, F32 = jnp.bfloat16, jnp.float32


def mm(x, y):
    return jnp.dot(x, y, preferred_element_type=F32)


def halves(x):
    hi = x.astype(BF)
    return hi, (x - hi.astype(F32)).astype(BF)


def selector(size, source):
    wanted = source(lax.broadcasted_iota(jnp.int32, (size, size), 0))
    return (wanted == lax.broadcasted_iota(jnp.int32, (size, size), 1)).astype(BF)


def pack_kernel(own_ref, far_ref, row_ref, col_ref, out_ref):
    pieces = [[] for _ in range(GRPS)]
    for ref in (own_ref, far_ref):
        total = 0.0
        for part in halves(ref[...] * SCALE):
            turned = mm(row_ref[...], part).astype(BF)
            total += mm(turned, col_ref[...])
        for q in range(OCC * OCC):
            for g in range(GRPS):
                pieces[g].append(
                    total[q * PAIRS : (q + 1) * PAIRS, g * TILE : (g + 1) * TILE]
                )
    for g in range(GRPS):
        out_ref[g] = jnp.concatenate(pieces[g], axis=1).astype(out_ref.dtype)


def unpack_kernel(grp_ref, live_ref, got_ref, own_ref, sum_ref, row_ref, col_ref, out_ref):
    zc = PAIRS // 2
    blocks = []
    for j in range(OCC):
        for xl in range(2):
            for i in range(OCC):
                q = i * OCC + j
                near, far = q * TILE, (OCC * OCC + q) * TILE
                blocks.append(
                    jnp.concatenate(
                        [
                            got_ref[g, xl, :, near : near + TILE].astype(F32)
                            + got_ref[g, 1 - xl, :, far : far + TILE].astype(F32)
                            for g in range(GRPS)
                        ],
                        axis=1,
                    )
                )
    stacked = jnp.concatenate(blocks, axis=0)
    total = 0.0
    for part in halves(stacked):
        turned = mm(row_ref[...], part).astype(BF)
        total += mm(turned, col_ref[...])
    summed = own_ref[...] + sum_ref[...] + total * (1 / SCALE)
    col = lax.broadcasted_iota(jnp.int32, summed.shape, 1)
    first = grp_ref[0] * SLAB + col // VB
    keep = (first < live_ref[0]) & (col % VB < live_ref[0])
    out_ref[...] = jnp.where(keep, summed, 0.0).astype(BF)


def on_device(amplitudes, integrals, live_counts):
    occ, nocc, k_all = amplitudes.shape
    shard, slab = integrals.shape
    rows, k_half = occ * nocc, k_all // 2
    xl = lax.axis_index("xl")
    pair = (xl * 8 + lax.axis_index("z")) * 2 + lax.axis_index("c")
    grp = lax.axis_index("y") * 2 + lax.axis_index("xh")

    at = pair * shard + jnp.arange(shard)
    live = (at // VB < live_counts[1]) & (at % VB < live_counts[1])
    w = jnp.where(live[:, None], integrals, 0)
    w_all = lax.all_gather(w, ("z", "c"), axis=0, tiled=True)

    t = amplitudes.reshape(rows, k_all)
    t_own = lax.dynamic_slice(t, (0, xl * k_half), (rows, k_half))
    t_out = lax.dynamic_slice(t, (0, (1 - xl) * k_half), (rows, k_half))
    up = [(i, (i + 1) % 4) for i in range(4)]
    down = [(i, (i - 1) % 4) for i in range(4)]
    t_far = jnp.concatenate(
        [
            lax.ppermute(t_out[: rows // 2], ("xh", "xl"), up),
            lax.ppermute(t_out[rows // 2 :], ("xh", "xl"), down),
        ],
        axis=0,
    )

    out_cols = selector(slab, lambda r: ((r // SLAB) % GRPS) * TILE + (r % SLAB) * SLAB + r // VB)
    in_cols = selector(slab, lambda r: ((r // SLAB) % SLAB) * VB + (r // TILE) * SLAB + r % SLAB)
    out_rows = selector(rows, lambda r: (r // nocc) * nocc + (r % PAIRS) * OCC + (r // PAIRS) % OCC)
    zc = PAIRS // 2
    in_rows = selector(rows, lambda r: (r // (zc * OCC)) * zc * OCC + (r % OCC) * zc + (r // OCC) % zc)

    p_own = mm(t_own, w_all)
    p_far = mm(t_far, w_all)
    fetched = lax.ppermute(p_far, "xl", [(0, 1), (1, 0)])

    params = pltpu.CompilerParams(vmem_limit_bytes=48 * 2**20)
    wire = pl.pallas_call(
        pack_kernel,
        out_shape=jax.ShapeDtypeStruct((GRPS, PAIRS, 2 * OCC * OCC * TILE), F32),
        compiler_params=params,
    )(p_own, p_far, out_rows, out_cols).astype(WIRE)
    got = lax.all_to_all(
        wire.reshape(GRPS * PAIRS, -1), ("y", "xh", "xl", "z", "c"), 0, 0, tiled=True
    )
    whole = pl.BlockSpec(memory_space=pltpu.VMEM)
    small = pl.BlockSpec(memory_space=pltpu.SMEM)
    out = pl.pallas_call(
        unpack_kernel,
        out_shape=jax.ShapeDtypeStruct((rows, slab), BF),
        in_specs=[small, small, whole, whole, whole, whole, whole],
        compiler_params=params,
    )(
        grp.reshape(1),
        live_counts,
        got.reshape(GRPS, 2, zc, -1).astype(F32),
        p_own,
        fetched,
        in_rows,
        in_cols,
    )
    return out.reshape(occ, nocc, slab)


def solution(mesh):
    fine = Mesh(mesh.devices.reshape(4, 2, 2, 8, 2), ("y", "xh", "xl", "z", "c"))
    pair, grp = ("xl", "z", "c"), ("y", "xh")
    return jax.shard_map(
        on_device,
        mesh=fine,
        in_specs=(P(pair, None, None), P(pair, grp), P()),
        out_specs=P(pair, None, grp),
        check_vma=False,
    )
```

```python
import jax
import jax.numpy as jnp
from jax import lax
from jax.experimental import pallas as pl
from jax.experimental.pallas import tpu as pltpu
from jax.sharding import Mesh
from jax.sharding import PartitionSpec as P

VB = 96
OCC = 3
GRPS = 8
PAIRS = 32
SLAB = VB // GRPS
PIECE = SLAB // 4 * SLAB
LANES = 384
WIRE = jnp.float16
SCALE = 16.0
BF, F32 = jnp.bfloat16, jnp.float32
ORDER = ("y", "xh", "xl", "c", "z")


def mm(x, y):
    return jnp.dot(x, y, preferred_element_type=F32)


def halves(x):
    hi = x.astype(BF)
    return hi, (x - hi.astype(F32)).astype(BF)


def selector(size, source):
    wanted = source(lax.broadcasted_iota(jnp.int32, (size, size), 0))
    return (wanted == lax.broadcasted_iota(jnp.int32, (size, size), 1)).astype(BF)


def pack_kernel(parts_ref, row_ref, col_ref, out_ref, turned_ref):
    rows = row_ref.shape[0]
    for o in range(4):
        total = 0.0
        for part in halves(parts_ref[o * rows : (o + 1) * rows] * SCALE):
            total += mm(mm(row_ref[...], part).astype(BF), col_ref[...])
        turned_ref[o] = total
    fill = jnp.zeros((PAIRS, LANES - OCC * OCC * PIECE), F32)
    for g in range(GRPS):
        planes = []
        for o in range(4):
            for a in range(2):
                at = (g * 2 + a) * PIECE
                cut = [
                    turned_ref[o, q * PAIRS : (q + 1) * PAIRS, at : at + PIECE]
                    for q in range(OCC * OCC)
                ]
                planes.append(jnp.concatenate([*cut, fill], axis=1))
        message = jnp.swapaxes(jnp.stack(planes, axis=0), 0, 1)
        out_ref[g * PAIRS : (g + 1) * PAIRS] = message


def unpack_kernel(
    place_ref, live_ref, got_ref, own_ref, near_ref, side_ref, row_ref, col_ref, out_ref, v_ref, s_ref
):
    for g in range(GRPS):
        message = got_ref[g * PAIRS : (g + 1) * PAIRS]
        v_ref[g] = jnp.swapaxes(message, 0, 1)
    for xl in range(2):
        for c in range(2):
            for g in range(GRPS):
                for cs in range(2):
                    for a in range(2):
                        oc = (c ^ cs) * 2 + a
                        near, far = (xl * 2 + cs) * 8, ((1 - xl) * 2 + cs) * 8
                        s_ref[xl * 2 + c, (g * 2 + cs) * 2 + a] = (
                            v_ref[g, oc, near : near + 8] + v_ref[g, 4 + oc, far : far + 8]
                        )
    blocks = []
    for j in range(OCC):
        for xc in range(4):
            for i in range(OCC):
                at = (i * OCC + j) * PIECE
                blocks.append(
                    jnp.concatenate(
                        [s_ref[xc, n, :, at : at + PIECE] for n in range(4 * GRPS)], axis=1
                    )
                )
    stacked = jnp.concatenate(blocks, axis=0)
    total = 0.0
    for part in halves(stacked):
        total += mm(mm(row_ref[...], part).astype(BF), col_ref[...])
    mine = own_ref[...] + near_ref[...]
    side = side_ref[...]
    first_core = place_ref[1] == 0
    direct = jnp.concatenate(
        [jnp.where(first_core, mine, side), jnp.where(first_core, side, mine)], axis=1
    )
    summed = direct + total * (1 / SCALE)
    col = lax.broadcasted_iota(jnp.int32, summed.shape, 1)
    first = place_ref[0] * SLAB + col // VB
    keep = (first < live_ref[0]) & (col % VB < live_ref[0])
    out_ref[...] = jnp.where(keep, summed, 0.0).astype(BF)


def gather(block):
    return lax.all_gather(block, "z", axis=0, tiled=True)


def on_device(amplitudes, integrals, live_counts):
    occ, nocc, k_all = amplitudes.shape
    shard, slab = integrals.shape
    rows, k_half, half = occ * nocc, k_all // 2, slab // 2
    xl, c = lax.axis_index("xl"), lax.axis_index("c")
    pair = (xl * 8 + lax.axis_index("z")) * 2 + c
    grp = lax.axis_index("y") * 2 + lax.axis_index("xh")
    swap = [(0, 1), (1, 0)]

    at = pair * shard + jnp.arange(shard)
    live = (at // VB < live_counts[1]) & (at % VB < live_counts[1])
    w = jnp.where(live[:, None], integrals, 0)
    w_keep = jnp.where(c == 0, w[:, :half], w[:, half:])
    w_send = jnp.where(c == 0, w[:, half:], w[:, :half])
    w_recv = lax.ppermute(w_send, "c", swap)
    block = jnp.where(
        c == 0,
        jnp.concatenate([w_keep, w_recv], axis=0),
        jnp.concatenate([w_recv, w_keep], axis=0),
    )
    w_all = gather(block)

    t = amplitudes.reshape(rows, k_all)
    t_own = lax.dynamic_slice(t, (0, xl * k_half), (rows, k_half))
    t_out = lax.dynamic_slice(t, (0, (1 - xl) * k_half), (rows, k_half))
    up = [(i, (i + 1) % 4) for i in range(4)]
    down = [(i, (i - 1) % 4) for i in range(4)]
    t_far = jnp.concatenate(
        [
            lax.ppermute(t_out[: rows // 2], ("xh", "xl"), up),
            lax.ppermute(t_out[rows // 2 :], ("xh", "xl"), down),
        ],
        axis=0,
    )
    near = jnp.concatenate([t_own, lax.ppermute(t_own, "c", swap)], axis=0)
    far = jnp.concatenate([t_far, lax.ppermute(t_far, "c", swap)], axis=0)

    zs = PAIRS // 4
    out_cols = selector(half, lambda r: ((r // SLAB) % GRPS) * (half // GRPS) + r // VB * SLAB + r % SLAB)
    in_cols = selector(slab, lambda r: (r % SLAB) * VB + r // SLAB)
    out_rows = selector(
        rows,
        lambda r: r // nocc * nocc
        + (r % PAIRS // 16) * 48
        + (r % zs) * 6
        + (r // zs % 2) * 3
        + r // PAIRS % OCC,
    )
    in_rows = selector(rows, lambda r: r // 48 * 48 + (r // 3 % 2) * 24 + (r % 3) * 8 + r // 6 % zs)

    p_near = mm(near, w_all)
    p_far = mm(far, w_all)
    fetched = lax.ppermute(p_far, "xl", swap)
    side = lax.ppermute(p_near[rows:] + fetched[rows:], "c", swap)

    params = pltpu.CompilerParams(vmem_limit_bytes=48 * 2**20)
    wire = pl.pallas_call(
        pack_kernel,
        out_shape=jax.ShapeDtypeStruct((GRPS * PAIRS, 8, LANES), F32),
        scratch_shapes=[pltpu.VMEM((4, rows, half), F32)],
        compiler_params=params,
    )(jnp.concatenate([p_near, p_far], axis=0), out_rows, out_cols).astype(WIRE)
    got = lax.all_to_all(wire, ORDER, 0, 0, tiled=True)
    whole = pl.BlockSpec(memory_space=pltpu.VMEM)
    small = pl.BlockSpec(memory_space=pltpu.SMEM)
    out = pl.pallas_call(
        unpack_kernel,
        out_shape=jax.ShapeDtypeStruct((rows, slab), BF),
        in_specs=[small, small] + [whole] * 6,
        scratch_shapes=[
            pltpu.VMEM((GRPS, 8, PAIRS, LANES), F32),
            pltpu.VMEM((4, 4 * GRPS, 8, LANES), F32),
        ],
        compiler_params=params,
    )(
        jnp.stack([grp, c]),
        live_counts,
        got.astype(F32),
        p_near[:rows],
        fetched[:rows],
        side,
        in_rows,
        in_cols,
    )
    return out.reshape(occ, nocc, slab)


def solution(mesh):
    fine = Mesh(mesh.devices.reshape(4, 2, 2, 8, 2), ("y", "xh", "xl", "z", "c"))
    pair, grp = ("xl", "z", "c"), ("y", "xh")
    return jax.shard_map(
        on_device,
        mesh=fine,
        in_specs=(P(pair, None, None), P(pair, grp), P()),
        out_specs=P(pair, None, grp),
        check_vma=False,
    )
```

```python
import jax
import jax.numpy as jnp
from jax import lax
from jax.experimental import pallas as pl
from jax.experimental.pallas import tpu as pltpu
from jax.sharding import Mesh
from jax.sharding import PartitionSpec as P

VB = 96
OCC = 3
GRPS = 8
PAIRS = 32
ZS = 8
SLAB = VB // GRPS
PIECE = SLAB // 4 * SLAB
LANES = 384
CHUNK = 1152
WIRE = jnp.float16
SCALE = 16.0
BF, F32 = jnp.bfloat16, jnp.float32
ORDER = ("y", "xh", "xl", "c", "z")
SWAP = [(0, 1), (1, 0)]


def mm(x, y):
    return jnp.dot(x, y, preferred_element_type=F32)


def halves(x):
    hi = x.astype(BF)
    return hi, (x - hi.astype(F32)).astype(BF)


def selector(size, source):
    wanted = source(lax.broadcasted_iota(jnp.int32, (size, size), 0))
    return (wanted == lax.broadcasted_iota(jnp.int32, (size, size), 1)).astype(BF)


def product_kernel(*refs):
    *t_refs, w_ref, row_ref, col_ref, ladder_ref, out_ref, turned_ref = refs
    step = pl.program_id(0)

    @pl.when(step == 0)
    def _():
        ladder_ref[...] = jnp.zeros_like(ladder_ref)

    at = 0
    for t_ref in t_refs:
        size = t_ref.shape[0]
        ladder_ref[at : at + size] += mm(t_ref[...], w_ref[...])
        at += size

    @pl.when(step == pl.num_programs(0) - 1)
    def _():
        rows = row_ref.shape[0]
        for o in range(4):
            total = 0.0
            for part in halves(ladder_ref[o * rows : (o + 1) * rows] * SCALE):
                total += mm(mm(row_ref[...], part).astype(BF), col_ref[...])
            turned_ref[o] = total
        fill = jnp.zeros((PAIRS, LANES - OCC * OCC * PIECE), F32)
        for g in range(GRPS):
            planes = []
            for o in range(4):
                cut = [
                    turned_ref[o, q * PAIRS : (q + 1) * PAIRS, g * PIECE : (g + 1) * PIECE]
                    for q in range(OCC * OCC)
                ]
                planes.append(jnp.concatenate([*cut, fill], axis=1))
            message = jnp.swapaxes(jnp.stack(planes, axis=0), 0, 1)
            out_ref[g * PAIRS : (g + 1) * PAIRS] = message


def unpack_kernel(
    place_ref, live_ref, got_ref, own_ref, side_ref, far_ref, row_ref, col_ref, out_ref, v_ref
):
    for g in range(GRPS):
        v_ref[g] = jnp.swapaxes(got_ref[g * PAIRS : (g + 1) * PAIRS], 0, 1)
    blocks = []
    for j in range(OCC):
        for xl in range(2):
            for c in range(2):
                for i in range(OCC):
                    at = (i * OCC + j) * PIECE
                    cut = []
                    for g in range(GRPS):
                        for xs in range(2):
                            for cs in range(2):
                                z = (xs * 2 + cs) * ZS
                                o = (xl ^ xs) * 2 + (c ^ cs)
                                cut.append(v_ref[g, o, z : z + ZS, at : at + PIECE])
                    blocks.append(jnp.concatenate(cut, axis=1))
    stacked = jnp.concatenate(blocks, axis=0)
    total = 0.0
    for part in halves(stacked):
        total += mm(mm(row_ref[...], part).astype(BF), col_ref[...])

    def joined(first, x, y):
        return jnp.where(
            first, jnp.concatenate([x, y], axis=1), jnp.concatenate([y, x], axis=1)
        )

    near = joined(place_ref[1] == 0, own_ref[...], side_ref[...])
    far = joined(place_ref[1] == 0, far_ref[0], far_ref[1])
    summed = joined(place_ref[2] == 0, near, far) + total * (1 / SCALE)
    col = lax.broadcasted_iota(jnp.int32, summed.shape, 1)
    first = place_ref[0] * SLAB + col // VB
    keep = (first < live_ref[0]) & (col % VB < live_ref[0])
    out_ref[...] = jnp.where(keep, summed, 0.0).astype(BF)


def shift(x, axis, size, by):
    return lax.ppermute(x, axis, [(i, (i + by) % size) for i in range(size)])


def ring(block):
    half = block.shape[0] // 2
    up, down = [block], [block]
    for _ in range(ZS // 2 - 1):
        up.append(shift(up[-1], "z", ZS, 1))
        down.append(shift(down[-1], "z", ZS, -1))
    pieces = [(k, 0, b) for k, b in enumerate(up)]
    pieces += [(-k, 0, b) for k, b in enumerate(down) if k]
    last = ZS // 2
    pieces.append((last, 0, shift(up[-1][:half], "z", ZS, 1)))
    pieces.append((-last, half, shift(down[-1][half:], "z", ZS, -1)))
    return pieces


def on_device(amplitudes, integrals, live_counts):
    occ, nocc, k_all = amplitudes.shape
    shard, slab = integrals.shape
    rows, k_half, half, quarter = occ * nocc, k_all // 2, slab // 2, slab // 4
    xl, z, c = lax.axis_index("xl"), lax.axis_index("z"), lax.axis_index("c")
    pair = (xl * ZS + z) * 2 + c
    grp = lax.axis_index("y") * 2 + lax.axis_index("xh")

    t = amplitudes.reshape(rows, k_all)
    t_up = shift(t[: rows // 2], ("xh", "xl"), 4, 1)
    t_down = shift(t[rows // 2 :], ("xh", "xl"), 4, -1)

    at = pair * shard + jnp.arange(shard)
    live = (at // VB < live_counts[1]) & (at % VB < live_counts[1])
    w = jnp.where(live[:, None], integrals, 0)
    cols = [w[:, n * quarter : (n + 1) * quarter] for n in range(4)]
    first = c == 0
    w_keep = jnp.concatenate(
        [jnp.where(first, cols[0], cols[1]), jnp.where(first, cols[2], cols[3])], axis=0
    )
    w_send = jnp.concatenate(
        [jnp.where(first, cols[1], cols[0]), jnp.where(first, cols[3], cols[2])], axis=0
    )
    w_side = lax.ppermute(w_send, "c", SWAP)
    both = []
    for n in range(2):
        keep, side = w_keep[n * shard : (n + 1) * shard], w_side[n * shard : (n + 1) * shard]
        both.append(
            jnp.where(
                first,
                jnp.concatenate([keep, side], axis=0),
                jnp.concatenate([side, keep], axis=0),
            )
        )
    near = jnp.where(xl == 0, both[0], both[1])
    far = lax.ppermute(jnp.where(xl == 0, both[1], both[0]), "xl", SWAP)

    w_all = jnp.zeros((k_all, quarter), BF)
    for block, base in ((near, xl * k_half), (far, (1 - xl) * k_half)):
        for back, row, piece in ring(block):
            start = base + (z - back) % ZS * (2 * shard) + row
            w_all = lax.dynamic_update_slice(w_all, piece, (start, 0))

    t_refs = [t, lax.ppermute(t, "c", SWAP), t_up, t_down]
    t_refs += [lax.ppermute(t_up, "c", SWAP), lax.ppermute(t_down, "c", SWAP)]

    out_cols = selector(quarter, lambda r: ((r // SLAB) % GRPS) * PIECE + r // VB * SLAB + r % SLAB)
    in_cols = selector(slab, lambda r: (r % SLAB) * VB + r // SLAB)
    out_rows = selector(
        rows,
        lambda r: r // nocc * nocc
        + (r % PAIRS // 16) * 48
        + (r % ZS) * 6
        + (r // ZS % 2) * 3
        + r // PAIRS % OCC,
    )
    in_rows = selector(rows, lambda r: r // 48 * 48 + (r // 3 % 2) * 24 + (r % 3) * 8 + r // 6 % ZS)

    params = pltpu.CompilerParams(vmem_limit_bytes=48 * 2**20)
    fixed = lambda k: (0, 0)
    ladder, wire = pl.pallas_call(
        product_kernel,
        grid=(k_all // CHUNK,),
        in_specs=[pl.BlockSpec((x.shape[0], CHUNK), lambda k: (0, k)) for x in t_refs]
        + [
            pl.BlockSpec((CHUNK, quarter), lambda k: (k, 0)),
            pl.BlockSpec((rows, rows), fixed),
            pl.BlockSpec((quarter, quarter), fixed),
        ],
        out_specs=[
            pl.BlockSpec((4 * rows, quarter), fixed),
            pl.BlockSpec((GRPS * PAIRS, 4, LANES), lambda k: (0, 0, 0)),
        ],
        out_shape=[
            jax.ShapeDtypeStruct((4 * rows, quarter), F32),
            jax.ShapeDtypeStruct((GRPS * PAIRS, 4, LANES), F32),
        ],
        scratch_shapes=[pltpu.VMEM((4, rows, quarter), F32)],
        compiler_params=params,
    )(*t_refs, w_all, out_rows, out_cols)

    parts = ladder.reshape(2, 2, rows, quarter)
    side = lax.ppermute(parts[:, 1], "c", SWAP)
    fetched = lax.ppermute(jnp.stack([parts[1, 0], side[1]]), "xl", SWAP)

    got = lax.all_to_all(wire.astype(WIRE), ORDER, 0, 0, tiled=True)
    whole = pl.BlockSpec(memory_space=pltpu.VMEM)
    small = pl.BlockSpec(memory_space=pltpu.SMEM)
    out = pl.pallas_call(
        unpack_kernel,
        out_shape=jax.ShapeDtypeStruct((rows, slab), BF),
        in_specs=[small, small] + [whole] * 6,
        scratch_shapes=[pltpu.VMEM((GRPS, 4, PAIRS, LANES), F32)],
        compiler_params=params,
    )(
        jnp.stack([grp, c, xl]),
        live_counts,
        got.astype(F32),
        parts[0, 0],
        side[0],
        fetched,
        in_rows,
        in_cols,
    )
    return out.reshape(occ, nocc, slab)


def solution(mesh):
    fine = Mesh(mesh.devices.reshape(4, 2, 2, 8, 2), ("y", "xh", "xl", "z", "c"))
    pair, grp = ("xl", "z", "c"), ("y", "xh")
    return jax.shard_map(
        on_device,
        mesh=fine,
        in_specs=(P(pair, None, None), P(pair, grp), P()),
        out_specs=P(pair, None, grp),
        check_vma=False,
    )
```

```python
import jax
import jax.numpy as jnp
import numpy as np
from jax import lax
from jax.experimental import pallas as pl
from jax.experimental.pallas import tpu as pltpu
from jax.sharding import Mesh
from jax.sharding import PartitionSpec as P

VB = 96
OCC = 3
GRPS = 8
PAIRS = 32
ZS = 8
SLAB = VB // GRPS
PIECE = SLAB // 4 * SLAB
LANES = 384
CHUNK = 2304
WIRE = jnp.float16
SCALE = 16.0
BF, F32 = jnp.bfloat16, jnp.float32
ORDER = ("y", "xh", "xl", "c", "z")
SWAP = [(0, 1), (1, 0)]
SPLIT = 208
RING = [(0, 0, 0), (1, 1, 0), (2, 2, 0), (3, 3, 0), (-1, 4, 0), (-2, 5, 0), (-3, 6, 0), (4, 7, 0), (4, 7, SPLIT)]


def mm(x, y):
    return jnp.dot(x, y, preferred_element_type=F32)


def halves(x):
    hi = x.astype(BF)
    return hi, (x - hi.astype(F32)).astype(BF)


def selector(size, source):
    rows = np.arange(size)
    chosen = np.zeros((size, size), np.float32)
    chosen[rows, source(rows)] = 1
    return jnp.asarray(chosen, BF)


def folded(block):
    tall, third = block.shape[0] // 4, block.shape[1] // 3
    rest = [block[3 * tall :, n * third : (n + 1) * third] for n in range(3)]
    return jnp.concatenate([block[: 3 * tall], jnp.concatenate(rest, axis=0)], axis=1)


def product_kernel(place_ref, *refs):
    t_refs, refs = refs[:6], refs[6:]
    pieces, refs = refs[: 2 * len(RING)], refs[2 * len(RING) :]
    row_ref, col_ref, ladder_ref, out_ref, turned_ref, stage_ref, w_ref, sem = refs
    step = pl.program_id(0)

    @pl.when(step == 0)
    def _():
        ladder_ref[...] = jnp.zeros_like(ladder_ref)
        copies = []
        for n, piece in enumerate(pieces):
            slot, row = n // len(RING) * ZS + RING[n % len(RING)][1], RING[n % len(RING)][2]
            copies.append(
                pltpu.make_async_copy(
                    piece, stage_ref.at[slot, pl.ds(row, piece.shape[0])], sem.at[n]
                )
            )
        for copy in copies:
            copy.start()
        for copy in copies:
            copy.wait()
        z, xl = place_ref[0], place_ref[1]
        tall, width = stage_ref.shape[1] // 3, w_ref.shape[1]
        for stream in range(2):
            base = lax.rem(xl + stream, 2) * ZS
            for back, slot, _ in RING[:ZS]:
                start = (base + lax.rem(z + ZS - back, ZS)) * (4 * tall)
                start = pl.multiple_of(start, 4 * tall)
                slot = stream * ZS + slot
                w_ref[pl.ds(start, 3 * tall)] = stage_ref[slot, :, :width]
                rest = [stage_ref[slot, n * tall : (n + 1) * tall, width:] for n in range(3)]
                w_ref[pl.ds(start + 3 * tall, tall)] = jnp.concatenate(rest, axis=1)

    at = 0
    for t_ref in t_refs:
        size = t_ref.shape[0]
        ladder_ref[at : at + size] += mm(t_ref[...], w_ref[pl.ds(pl.multiple_of(step * CHUNK, CHUNK), CHUNK)])
        at += size

    @pl.when(step == pl.num_programs(0) - 1)
    def _():
        rows = row_ref.shape[0]
        for o in range(4):
            total = 0.0
            for part in halves(ladder_ref[o * rows : (o + 1) * rows] * SCALE):
                total += mm(mm(row_ref[...], part).astype(BF), col_ref[...])
            turned_ref[o] = total
        fill = jnp.zeros((PAIRS, LANES - OCC * OCC * PIECE), F32)
        for g in range(GRPS):
            planes = []
            for o in range(4):
                cut = [
                    turned_ref[o, q * PAIRS : (q + 1) * PAIRS, g * PIECE : (g + 1) * PIECE]
                    for q in range(OCC * OCC)
                ]
                planes.append(jnp.concatenate([*cut, fill], axis=1))
            message = jnp.swapaxes(jnp.stack(planes, axis=0), 0, 1)
            out_ref[g * PAIRS : (g + 1) * PAIRS] = message


def unpack_kernel(
    place_ref, live_ref, got_ref, own_ref, side_ref, far_ref, row_ref, col_ref, out_ref, v_ref
):
    for g in range(GRPS):
        v_ref[g] = jnp.swapaxes(got_ref[g * PAIRS : (g + 1) * PAIRS], 0, 1)
    blocks = []
    for j in range(OCC):
        for xl in range(2):
            for c in range(2):
                for i in range(OCC):
                    at = (i * OCC + j) * PIECE
                    cut = []
                    for g in range(GRPS):
                        for xs in range(2):
                            for cs in range(2):
                                z = (xs * 2 + cs) * ZS
                                o = (xl ^ xs) * 2 + (c ^ cs)
                                cut.append(v_ref[g, o, z : z + ZS, at : at + PIECE])
                    blocks.append(jnp.concatenate(cut, axis=1))
    stacked = jnp.concatenate(blocks, axis=0)
    total = 0.0
    for part in halves(stacked):
        total += mm(mm(row_ref[...], part).astype(BF), col_ref[...])

    def joined(first, x, y):
        return jnp.where(
            first, jnp.concatenate([x, y], axis=1), jnp.concatenate([y, x], axis=1)
        )

    near = joined(place_ref[1] == 0, own_ref[...], side_ref[...])
    far = joined(place_ref[1] == 0, far_ref[0], far_ref[1])
    summed = joined(place_ref[2] == 0, near, far) + total * (1 / SCALE)
    col = lax.broadcasted_iota(jnp.int32, summed.shape, 1)
    first = place_ref[0] * SLAB + col // VB
    keep = (first < live_ref[0]) & (col % VB < live_ref[0])
    out_ref[...] = jnp.where(keep, summed, 0.0).astype(BF)


def shift(x, axis, size, by):
    return lax.ppermute(x, axis, [(i, (i + by) % size) for i in range(size)])


def ring(block):
    up, down = [block], [block]
    for _ in range(ZS // 2 - 1):
        up.append(shift(up[-1], "z", ZS, 1))
        down.append(shift(down[-1], "z", ZS, -1))
    last = [shift(up[-1][:SPLIT], "z", ZS, 1), shift(down[-1][SPLIT:], "z", ZS, -1)]
    return up + down[1:] + last


def on_device(amplitudes, integrals, live_counts):
    occ, nocc, k_all = amplitudes.shape
    shard, slab = integrals.shape
    rows, quarter = occ * nocc, slab // 4
    xl, z, c = lax.axis_index("xl"), lax.axis_index("z"), lax.axis_index("c")
    pair = (xl * ZS + z) * 2 + c
    grp = lax.axis_index("y") * 2 + lax.axis_index("xh")

    at = pair * shard + jnp.arange(shard)
    live = (at // VB < live_counts[1]) & (at % VB < live_counts[1])
    w = jnp.where(live[:, None], integrals, 0)
    cols = [w[:, n * quarter : (n + 1) * quarter] for n in range(4)]
    first = c == 0
    w_keep = jnp.concatenate(
        [jnp.where(first, cols[0], cols[1]), jnp.where(first, cols[2], cols[3])], axis=0
    )
    w_send = jnp.concatenate(
        [jnp.where(first, cols[1], cols[0]), jnp.where(first, cols[3], cols[2])], axis=0
    )
    w_side = lax.ppermute(w_send, "c", SWAP)
    both = []
    for n in range(2):
        keep, side = w_keep[n * shard : (n + 1) * shard], w_side[n * shard : (n + 1) * shard]
        both.append(
            jnp.where(
                first,
                jnp.concatenate([keep, side], axis=0),
                jnp.concatenate([side, keep], axis=0),
            )
        )
    near = jnp.where(xl == 0, both[0], both[1])
    far = lax.ppermute(folded(jnp.where(xl == 0, both[1], both[0])), "xl", SWAP)
    pieces = ring(folded(near)) + ring(far)

    t = amplitudes.reshape(rows, k_all)
    t_low, t_high, _ = lax.optimization_barrier((t[: rows // 2], t[rows // 2 :], far))
    t_up = shift(t_low, ("xh", "xl"), 4, 1)
    t_down = shift(t_high, ("xh", "xl"), 4, -1)
    t_refs = [t, lax.ppermute(t, "c", SWAP), t_up, t_down]
    t_refs += [lax.ppermute(t_up, "c", SWAP), lax.ppermute(t_down, "c", SWAP)]

    out_cols = selector(quarter, lambda r: ((r // SLAB) % GRPS) * PIECE + r // VB * SLAB + r % SLAB)
    in_cols = selector(slab, lambda r: (r % SLAB) * VB + r // SLAB)
    out_rows = selector(
        rows,
        lambda r: r // nocc * nocc
        + (r % PAIRS // 16) * 48
        + (r % ZS) * 6
        + (r // ZS % 2) * 3
        + r // PAIRS % OCC,
    )
    in_rows = selector(rows, lambda r: r // 48 * 48 + (r // 3 % 2) * 24 + (r % 3) * 8 + r // 6 % ZS)

    params = pltpu.CompilerParams(vmem_limit_bytes=48 * 2**20)
    fixed = lambda k: (0, 0)
    ladder, wire = pl.pallas_call(
        product_kernel,
        grid=(k_all // CHUNK,),
        in_specs=[pl.BlockSpec(memory_space=pltpu.SMEM)]
        + [pl.BlockSpec((x.shape[0], CHUNK), lambda k: (0, k)) for x in t_refs]
        + [pl.BlockSpec(memory_space=pl.ANY)] * len(pieces)
        + [
            pl.BlockSpec((rows, rows), fixed),
            pl.BlockSpec((quarter, quarter), fixed),
        ],
        out_specs=[
            pl.BlockSpec((4 * rows, quarter), fixed),
            pl.BlockSpec((GRPS * PAIRS, 4, LANES), lambda k: (0, 0, 0)),
        ],
        out_shape=[
            jax.ShapeDtypeStruct((4 * rows, quarter), F32),
            jax.ShapeDtypeStruct((GRPS * PAIRS, 4, LANES), F32),
        ],
        scratch_shapes=[
            pltpu.VMEM((4, rows, quarter), F32),
            pltpu.VMEM((2 * ZS, *far.shape), BF),
            pltpu.VMEM((k_all, quarter), BF),
            pltpu.SemaphoreType.DMA((len(pieces),)),
        ],
        compiler_params=params,
    )(jnp.stack([z, xl]), *t_refs, *pieces, out_rows, out_cols)

    parts = ladder.reshape(2, 2, rows, quarter)
    side = lax.ppermute(parts[:, 1], "c", SWAP)
    fetched = lax.ppermute(jnp.stack([parts[1, 0], side[1]]), "xl", SWAP)

    got = lax.all_to_all(wire.astype(WIRE), ORDER, 0, 0, tiled=True)
    whole = pl.BlockSpec(memory_space=pltpu.VMEM)
    small = pl.BlockSpec(memory_space=pltpu.SMEM)
    out = pl.pallas_call(
        unpack_kernel,
        out_shape=jax.ShapeDtypeStruct((rows, slab), BF),
        in_specs=[small, small] + [whole] * 6,
        scratch_shapes=[pltpu.VMEM((GRPS, 4, PAIRS, LANES), F32)],
        compiler_params=params,
    )(
        jnp.stack([grp, c, xl]),
        live_counts,
        got.astype(F32),
        parts[0, 0],
        side[0],
        fetched,
        in_rows,
        in_cols,
    )
    return out.reshape(occ, nocc, slab)


def solution(mesh):
    fine = Mesh(mesh.devices.reshape(4, 2, 2, 8, 2), ("y", "xh", "xl", "z", "c"))
    pair, grp = ("xl", "z", "c"), ("y", "xh")
    return jax.shard_map(
        on_device,
        mesh=fine,
        in_specs=(P(pair, None, None), P(pair, grp), P()),
        out_specs=P(pair, None, grp),
        check_vma=False,
    )
```

```python
import jax
import jax.numpy as jnp
import numpy as np
from jax import lax
from jax.experimental import pallas as pl
from jax.experimental.pallas import tpu as pltpu
from jax.sharding import Mesh
from jax.sharding import PartitionSpec as P

VB = 96
OCC = 3
GRPS = 8
PAIRS = 32
ZS = 8
SLAB = VB // GRPS
PIECE = SLAB // 4 * SLAB
LANES = 384
CHUNK = 2304
WIRE = jnp.float16
SCALE = 16.0
BF, F32 = jnp.bfloat16, jnp.float32
ORDER = ("y", "xh", "xl", "c", "z")
SWAP = [(0, 1), (1, 0)]


def mm(x, y):
    return jnp.dot(x, y, preferred_element_type=F32)


def halves(x):
    hi = x.astype(BF)
    return hi, (x - hi.astype(F32)).astype(BF)


def selector(size, source):
    rows = np.arange(size)
    chosen = np.zeros((size, size), np.float32)
    chosen[rows, source(rows)] = 1
    return jnp.asarray(chosen, BF)


def folded(block):
    tall, third = block.shape[0] // 4, block.shape[1] // 3
    rest = [block[3 * tall :, n * third : (n + 1) * third] for n in range(3)]
    return jnp.concatenate([block[: 3 * tall], jnp.concatenate(rest, axis=0)], axis=1)


def product_kernel(place_ref, *refs):
    t_refs, pieces, refs = refs[:4], refs[4 : 4 + 2 * ZS], refs[4 + 2 * ZS :]
    row_ref, col_ref, ladder_ref, out_ref, turned_ref, stage_ref, w_ref, sem = refs
    step = pl.program_id(0)

    @pl.when(step == 0)
    def _():
        ladder_ref[...] = jnp.zeros_like(ladder_ref)
        copies = [
            pltpu.make_async_copy(piece, stage_ref.at[n], sem.at[n])
            for n, piece in enumerate(pieces)
        ]
        for copy in copies:
            copy.start()
        for copy in copies:
            copy.wait()
        z, xl, c = place_ref[0], place_ref[1], place_ref[2]
        tall, width = stage_ref.shape[1] // 3, w_ref.shape[1]
        for n in range(2 * ZS):
            k = n % ZS
            back = jnp.where(c == 0, k, ZS - k)
            of = jnp.where(n < ZS, xl, 1 - xl) * ZS + lax.rem(z + ZS - back, ZS)
            start = pl.multiple_of(of * (4 * tall), 4 * tall)
            w_ref[pl.ds(start, 3 * tall)] = stage_ref[n, :, :width]
            rest = [stage_ref[n, m * tall : (m + 1) * tall, width:] for m in range(3)]
            w_ref[pl.ds(start + 3 * tall, tall)] = jnp.concatenate(rest, axis=1)

    at = 0
    for t_ref in t_refs:
        size = t_ref.shape[0]
        ladder_ref[at : at + size] += mm(t_ref[...], w_ref[pl.ds(pl.multiple_of(step * CHUNK, CHUNK), CHUNK)])
        at += size

    @pl.when(step == pl.num_programs(0) - 1)
    def _():
        rows = row_ref.shape[0]
        for o in range(4):
            total = 0.0
            for part in halves(ladder_ref[o * rows : (o + 1) * rows] * SCALE):
                total += mm(mm(row_ref[...], part).astype(BF), col_ref[...])
            turned_ref[o] = total
        fill = jnp.zeros((PAIRS, LANES - OCC * OCC * PIECE), F32)
        for g in range(GRPS):
            planes = []
            for o in range(4):
                cut = [
                    turned_ref[o, q * PAIRS : (q + 1) * PAIRS, g * PIECE : (g + 1) * PIECE]
                    for q in range(OCC * OCC)
                ]
                planes.append(jnp.concatenate([*cut, fill], axis=1))
            message = jnp.swapaxes(jnp.stack(planes, axis=0), 0, 1)
            out_ref[g * PAIRS : (g + 1) * PAIRS] = message


def unpack_kernel(
    place_ref, live_ref, got_ref, own_ref, side_ref, far_ref, row_ref, col_ref, out_ref, v_ref
):
    for g in range(GRPS):
        v_ref[g] = jnp.swapaxes(got_ref[g * PAIRS : (g + 1) * PAIRS], 0, 1)
    blocks = []
    for j in range(OCC):
        for xl in range(2):
            for c in range(2):
                for i in range(OCC):
                    at = (i * OCC + j) * PIECE
                    cut = []
                    for g in range(GRPS):
                        for xs in range(2):
                            for cs in range(2):
                                z = (xs * 2 + cs) * ZS
                                o = (xl ^ xs) * 2 + (c ^ cs)
                                cut.append(v_ref[g, o, z : z + ZS, at : at + PIECE])
                    blocks.append(jnp.concatenate(cut, axis=1))
    stacked = jnp.concatenate(blocks, axis=0)
    total = 0.0
    for part in halves(stacked):
        total += mm(mm(row_ref[...], part).astype(BF), col_ref[...])

    def joined(first, x, y):
        return jnp.where(
            first, jnp.concatenate([x, y], axis=1), jnp.concatenate([y, x], axis=1)
        )

    near = joined(place_ref[1] == 0, own_ref[...], side_ref[...])
    far = joined(place_ref[1] == 0, far_ref[0], far_ref[1])
    summed = joined(place_ref[2] == 0, near, far) + total * (1 / SCALE)
    col = lax.broadcasted_iota(jnp.int32, summed.shape, 1)
    first = place_ref[0] * SLAB + col // VB
    keep = (first < live_ref[0]) & (col % VB < live_ref[0])
    out_ref[...] = jnp.where(keep, summed, 0.0).astype(BF)


def around(x, axes, size):
    moves = [(i * 2, (i + 1) % size * 2) for i in range(size)]
    moves += [(i * 2 + 1, (i - 1) % size * 2 + 1) for i in range(size)]
    return lax.ppermute(x, (*axes, "c"), moves)


def ring(block):
    blocks = [block]
    for _ in range(ZS - 1):
        blocks.append(around(blocks[-1], ("z",), ZS))
    return blocks


def on_device(amplitudes, integrals, live_counts):
    occ, nocc, k_all = amplitudes.shape
    shard, slab = integrals.shape
    rows, quarter = occ * nocc, slab // 4
    xl, z, c = lax.axis_index("xl"), lax.axis_index("z"), lax.axis_index("c")
    pair = (xl * ZS + z) * 2 + c
    grp = lax.axis_index("y") * 2 + lax.axis_index("xh")

    at = pair * shard + jnp.arange(shard)
    live = (at // VB < live_counts[1]) & (at % VB < live_counts[1])
    w = jnp.where(live[:, None], integrals, 0)
    cols = [w[:, n * quarter : (n + 1) * quarter] for n in range(4)]
    first = c == 0
    w_keep = jnp.concatenate(
        [jnp.where(first, cols[0], cols[1]), jnp.where(first, cols[2], cols[3])], axis=0
    )
    w_send = jnp.concatenate(
        [jnp.where(first, cols[1], cols[0]), jnp.where(first, cols[3], cols[2])], axis=0
    )
    w_side = lax.ppermute(w_send, "c", SWAP)
    both = []
    for n in range(2):
        keep, side = w_keep[n * shard : (n + 1) * shard], w_side[n * shard : (n + 1) * shard]
        both.append(
            jnp.where(
                first,
                jnp.concatenate([keep, side], axis=0),
                jnp.concatenate([side, keep], axis=0),
            )
        )
    near = jnp.where(xl == 0, both[0], both[1])
    far = lax.ppermute(folded(jnp.where(xl == 0, both[1], both[0])), "xl", SWAP)
    ring_near, ring_far = ring(folded(near)), ring(far)
    pieces = ring_near + ring_far

    t, _ = lax.optimization_barrier((amplitudes.reshape(rows, k_all), (far, ring_near[1])))
    t_x = around(t, ("xh", "xl"), 4)
    t_x, *_ = lax.optimization_barrier((t_x, ring_near[-1], ring_far[-1]))
    t_refs = [t, lax.ppermute(t, "c", SWAP), t_x, lax.ppermute(t_x, "c", SWAP)]

    out_cols = selector(quarter, lambda r: ((r // SLAB) % GRPS) * PIECE + r // VB * SLAB + r % SLAB)
    in_cols = selector(slab, lambda r: (r % SLAB) * VB + r // SLAB)
    out_rows = selector(
        rows,
        lambda r: r // nocc * nocc
        + (r % PAIRS // 16) * 48
        + (r % ZS) * 6
        + (r // ZS % 2) * 3
        + r // PAIRS % OCC,
    )
    in_rows = selector(rows, lambda r: r // 48 * 48 + (r // 3 % 2) * 24 + (r % 3) * 8 + r // 6 % ZS)

    params = pltpu.CompilerParams(vmem_limit_bytes=48 * 2**20)
    fixed = lambda k: (0, 0)
    ladder, wire = pl.pallas_call(
        product_kernel,
        grid=(k_all // CHUNK,),
        in_specs=[pl.BlockSpec(memory_space=pltpu.SMEM)]
        + [pl.BlockSpec((x.shape[0], CHUNK), lambda k: (0, k)) for x in t_refs]
        + [pl.BlockSpec(memory_space=pl.ANY)] * len(pieces)
        + [
            pl.BlockSpec((rows, rows), fixed),
            pl.BlockSpec((quarter, quarter), fixed),
        ],
        out_specs=[
            pl.BlockSpec((4 * rows, quarter), fixed),
            pl.BlockSpec((GRPS * PAIRS, 4, LANES), lambda k: (0, 0, 0)),
        ],
        out_shape=[
            jax.ShapeDtypeStruct((4 * rows, quarter), F32),
            jax.ShapeDtypeStruct((GRPS * PAIRS, 4, LANES), F32),
        ],
        scratch_shapes=[
            pltpu.VMEM((4, rows, quarter), F32),
            pltpu.VMEM((2 * ZS, *far.shape), BF),
            pltpu.VMEM((k_all, quarter), BF),
            pltpu.SemaphoreType.DMA((len(pieces),)),
        ],
        compiler_params=params,
    )(jnp.stack([z, xl, c]), *t_refs, *pieces, out_rows, out_cols)

    parts = ladder.reshape(2, 2, rows, quarter)
    side = lax.ppermute(parts[:, 1], "c", SWAP)
    fetched = lax.ppermute(jnp.stack([parts[1, 0], side[1]]), "xl", SWAP)

    got = lax.all_to_all(wire.astype(WIRE), ORDER, 0, 0, tiled=True)
    whole = pl.BlockSpec(memory_space=pltpu.VMEM)
    small = pl.BlockSpec(memory_space=pltpu.SMEM)
    out = pl.pallas_call(
        unpack_kernel,
        out_shape=jax.ShapeDtypeStruct((rows, slab), BF),
        in_specs=[small, small] + [whole] * 6,
        scratch_shapes=[pltpu.VMEM((GRPS, 4, PAIRS, LANES), F32)],
        compiler_params=params,
    )(
        jnp.stack([grp, c, xl]),
        live_counts,
        got.astype(F32),
        parts[0, 0],
        side[0],
        fetched,
        in_rows,
        in_cols,
    )
    return out.reshape(occ, nocc, slab)


def solution(mesh):
    fine = Mesh(mesh.devices.reshape(4, 2, 2, 8, 2), ("y", "xh", "xl", "z", "c"))
    pair, grp = ("xl", "z", "c"), ("y", "xh")
    return jax.shard_map(
        on_device,
        mesh=fine,
        in_specs=(P(pair, None, None), P(pair, grp), P()),
        out_specs=P(pair, None, grp),
        check_vma=False,
    )
```

```python
import jax
import jax.numpy as jnp
import numpy as np
from jax import lax
from jax.experimental import pallas as pl
from jax.experimental.pallas import tpu as pltpu
from jax.sharding import Mesh
from jax.sharding import PartitionSpec as P

VB = 96
OCC = 3
GRPS = 8
PAIRS = 32
ZS = 8
SLAB = VB // GRPS
PIECE = SLAB // 4 * SLAB
LANES = 384
CHUNK = 2304
WIRE = jnp.float16
SCALE = 16.0
BF, F32 = jnp.bfloat16, jnp.float32
ORDER = ("y", "xh", "xl", "c", "z")
SWAP = [(0, 1), (1, 0)]


def mm(x, y):
    return jnp.dot(x, y, preferred_element_type=F32)


def halves(x):
    hi = x.astype(BF)
    return hi, (x - hi.astype(F32)).astype(BF)


def selector(size, source):
    rows = np.arange(size)
    chosen = np.zeros((size, size), np.float32)
    chosen[rows, source(rows)] = 1
    return jnp.asarray(chosen, BF)


def folded(block):
    tall, third = block.shape[0] // 4, block.shape[1] // 3
    rest = [block[3 * tall :, n * third : (n + 1) * third] for n in range(3)]
    return jnp.concatenate([block[: 3 * tall], jnp.concatenate(rest, axis=0)], axis=1)


def product_kernel(place_ref, *refs):
    t_refs, pieces, refs = refs[:6], refs[6 : 6 + 2 * ZS], refs[6 + 2 * ZS :]
    row_ref, col_ref, ladder_ref, out_ref, acc_ref, turned_ref, stage_ref, w_ref, sem = refs
    step = pl.program_id(0)

    @pl.when(step == 0)
    def _():
        acc_ref[...] = jnp.zeros_like(acc_ref)
        copies = [
            pltpu.make_async_copy(piece, stage_ref.at[n], sem.at[n])
            for n, piece in enumerate(pieces)
        ]
        for copy in copies:
            copy.start()
        for copy in copies:
            copy.wait()
        z, xl, c = place_ref[0], place_ref[1], place_ref[2]
        tall, width = stage_ref.shape[1] // 3, w_ref.shape[1]
        for n in range(2 * ZS):
            k = n % ZS
            back = jnp.where(c == 0, k, ZS - k)
            of = jnp.where(n < ZS, xl, 1 - xl) * ZS + lax.rem(z + ZS - back, ZS)
            start = pl.multiple_of(of * (4 * tall), 4 * tall)
            w_ref[pl.ds(start, 3 * tall)] = stage_ref[n, :, :width]
            rest = [stage_ref[n, m * tall : (m + 1) * tall, width:] for m in range(3)]
            w_ref[pl.ds(start + 3 * tall, tall)] = jnp.concatenate(rest, axis=1)

    w = w_ref[pl.ds(pl.multiple_of(step * CHUNK, CHUNK), CHUNK)]

    def add(*t_refs):
        t = jnp.concatenate([t_ref[...] for t_ref in t_refs], axis=0)
        acc_ref[...] += lax.dot_general(w, t, (((0,), (1,)), ((), ())), preferred_element_type=F32)

    early = step < pl.num_programs(0) // 2

    @pl.when(early)
    def _():
        add(*t_refs[:4])

    @pl.when(jnp.logical_not(early))
    def _():
        add(*t_refs[:2], *t_refs[4:])

    @pl.when(step == pl.num_programs(0) - 1)
    def _():
        ladder_ref[...] = acc_ref[...].T
        rows = row_ref.shape[0]
        for o in range(4):
            total = 0.0
            for part in halves(ladder_ref[o * rows : (o + 1) * rows] * SCALE):
                total += mm(mm(row_ref[...], part).astype(BF), col_ref[...])
            turned_ref[o] = total
        fill = jnp.zeros((PAIRS, LANES - OCC * OCC * PIECE), F32)
        for g in range(GRPS):
            planes = []
            for o in range(4):
                cut = [
                    turned_ref[o, q * PAIRS : (q + 1) * PAIRS, g * PIECE : (g + 1) * PIECE]
                    for q in range(OCC * OCC)
                ]
                planes.append(jnp.concatenate([*cut, fill], axis=1))
            message = jnp.swapaxes(jnp.stack(planes, axis=0), 0, 1)
            out_ref[g * PAIRS : (g + 1) * PAIRS] = message


def unpack_kernel(
    place_ref, live_ref, got_ref, own_ref, side_ref, far_ref, row_ref, col_ref, out_ref, v_ref
):
    for g in range(GRPS):
        v_ref[g] = jnp.swapaxes(got_ref[g * PAIRS : (g + 1) * PAIRS], 0, 1)
    blocks = []
    for j in range(OCC):
        for xl in range(2):
            for c in range(2):
                for i in range(OCC):
                    at = (i * OCC + j) * PIECE
                    cut = []
                    for g in range(GRPS):
                        for xs in range(2):
                            for cs in range(2):
                                z = (xs * 2 + cs) * ZS
                                o = (xl ^ xs) * 2 + (c ^ cs)
                                cut.append(v_ref[g, o, z : z + ZS, at : at + PIECE])
                    blocks.append(jnp.concatenate(cut, axis=1))
    stacked = jnp.concatenate(blocks, axis=0)
    total = 0.0
    for part in halves(stacked):
        total += mm(mm(row_ref[...], part).astype(BF), col_ref[...])

    def joined(first, x, y):
        return jnp.where(
            first, jnp.concatenate([x, y], axis=1), jnp.concatenate([y, x], axis=1)
        )

    near = joined(place_ref[1] == 0, own_ref[...], side_ref[0])
    far = joined(place_ref[1] == 0, far_ref[...], side_ref[1])
    summed = joined(place_ref[2] == 0, near, far) + total * (1 / SCALE)
    col = lax.broadcasted_iota(jnp.int32, summed.shape, 1)
    first = place_ref[0] * SLAB + col // VB
    keep = (first < live_ref[0]) & (col % VB < live_ref[0])
    out_ref[...] = jnp.where(keep, summed, 0.0).astype(BF)


def around(x, axes, size):
    moves = [(i * 2, (i + 1) % size * 2) for i in range(size)]
    moves += [(i * 2 + 1, (i - 1) % size * 2 + 1) for i in range(size)]
    return lax.ppermute(x, (*axes, "c"), moves)


def ring(block):
    blocks = [block]
    for _ in range(ZS - 1):
        blocks.append(around(blocks[-1], ("z",), ZS))
    return blocks


def on_device(amplitudes, integrals, live_counts):
    occ, nocc, k_all = amplitudes.shape
    shard, slab = integrals.shape
    rows, quarter = occ * nocc, slab // 4
    xl, z, c = lax.axis_index("xl"), lax.axis_index("z"), lax.axis_index("c")
    pair = (xl * ZS + z) * 2 + c
    grp = lax.axis_index("y") * 2 + lax.axis_index("xh")

    at = pair * shard + jnp.arange(shard)
    live = (at // VB < live_counts[1]) & (at % VB < live_counts[1])
    w = jnp.where(live[:, None], integrals, 0)
    cols = [w[:, n * quarter : (n + 1) * quarter] for n in range(4)]
    first = c == 0
    w_keep = jnp.concatenate(
        [jnp.where(first, cols[0], cols[1]), jnp.where(first, cols[2], cols[3])], axis=0
    )
    w_send = jnp.concatenate(
        [jnp.where(first, cols[1], cols[0]), jnp.where(first, cols[3], cols[2])], axis=0
    )
    w_side = lax.ppermute(w_send, "c", SWAP)
    both = []
    for n in range(2):
        keep, side = w_keep[n * shard : (n + 1) * shard], w_side[n * shard : (n + 1) * shard]
        both.append(
            jnp.where(
                first,
                jnp.concatenate([keep, side], axis=0),
                jnp.concatenate([side, keep], axis=0),
            )
        )
    near = jnp.where(xl == 0, both[0], both[1])
    far = lax.ppermute(folded(jnp.where(xl == 0, both[1], both[0])), "xl", SWAP)
    ring_near, ring_far = ring(folded(near)), ring(far)
    pieces = ring_near + ring_far

    t = amplitudes.reshape(rows, k_all)
    t_a, t_b, _ = lax.optimization_barrier(
        (t[:, : k_all // 2], t[:, k_all // 2 :], (far, ring_near[1]))
    )
    x_a, x_b = around(t_a, ("xh", "xl"), 4), around(t_b, ("xh", "xl"), 4)
    x_a, *_ = lax.optimization_barrier((x_a, ring_near[5], ring_far[4]))
    x_b, *_ = lax.optimization_barrier((x_b, ring_near[-1], ring_far[-1]))
    t_c, c_a, c_b = (lax.ppermute(x, "c", SWAP) for x in (t, x_a, x_b))
    t_refs = [t, t_c, x_a, c_a, x_b, c_b]

    out_cols = selector(quarter, lambda r: ((r // SLAB) % GRPS) * PIECE + r // VB * SLAB + r % SLAB)
    in_cols = selector(slab, lambda r: (r % SLAB) * VB + r // SLAB)
    out_rows = selector(
        rows,
        lambda r: r // nocc * nocc
        + (r % PAIRS // 16) * 48
        + (r % ZS) * 6
        + (r // ZS % 2) * 3
        + r // PAIRS % OCC,
    )
    in_rows = selector(rows, lambda r: r // 48 * 48 + (r // 3 % 2) * 24 + (r % 3) * 8 + r // 6 % ZS)

    params = pltpu.CompilerParams(vmem_limit_bytes=48 * 2**20)
    half = k_all // CHUNK // 2
    fixed = lambda k: (0, 0)
    full = lambda k: (0, k)
    early = lambda k: (0, jnp.minimum(k, half - 1))
    late = lambda k: (0, jnp.maximum(k - half, 0))
    ladder, wire = pl.pallas_call(
        product_kernel,
        grid=(k_all // CHUNK,),
        in_specs=[pl.BlockSpec(memory_space=pltpu.SMEM)]
        + [pl.BlockSpec((rows, CHUNK), chunk) for chunk in (full, full, early, early, late, late)]
        + [pl.BlockSpec(memory_space=pl.ANY)] * len(pieces)
        + [
            pl.BlockSpec((rows, rows), fixed),
            pl.BlockSpec((quarter, quarter), fixed),
        ],
        out_specs=[
            pl.BlockSpec((4 * rows, quarter), fixed),
            pl.BlockSpec((GRPS * PAIRS, 4, LANES), lambda k: (0, 0, 0)),
        ],
        out_shape=[
            jax.ShapeDtypeStruct((4 * rows, quarter), F32),
            jax.ShapeDtypeStruct((GRPS * PAIRS, 4, LANES), F32),
        ],
        scratch_shapes=[
            pltpu.VMEM((quarter, 4 * rows), F32),
            pltpu.VMEM((4, rows, quarter), F32),
            pltpu.VMEM((2 * ZS, *far.shape), BF),
            pltpu.VMEM((k_all, quarter), BF),
            pltpu.SemaphoreType.DMA((len(pieces),)),
        ],
        compiler_params=params,
    )(jnp.stack([z, xl, c]), *t_refs, *pieces, out_rows, out_cols)

    parts = ladder.reshape(2, 2, rows, quarter)
    fetched = lax.ppermute(parts[1], "xl", SWAP)
    side = lax.ppermute(jnp.stack([parts[0, 1], fetched[1]]), "c", SWAP)

    got = lax.all_to_all(wire.astype(WIRE), ORDER, 0, 0, tiled=True)
    whole = pl.BlockSpec(memory_space=pltpu.VMEM)
    small = pl.BlockSpec(memory_space=pltpu.SMEM)
    out = pl.pallas_call(
        unpack_kernel,
        out_shape=jax.ShapeDtypeStruct((rows, slab), BF),
        in_specs=[small, small] + [whole] * 6,
        scratch_shapes=[pltpu.VMEM((GRPS, 4, PAIRS, LANES), F32)],
        compiler_params=params,
    )(
        jnp.stack([grp, c, xl]),
        live_counts,
        got.astype(F32),
        parts[0, 0],
        side,
        fetched[0],
        in_rows,
        in_cols,
    )
    return out.reshape(occ, nocc, slab)


def solution(mesh):
    fine = Mesh(mesh.devices.reshape(4, 2, 2, 8, 2), ("y", "xh", "xl", "z", "c"))
    pair, grp = ("xl", "z", "c"), ("y", "xh")
    return jax.shard_map(
        on_device,
        mesh=fine,
        in_specs=(P(pair, None, None), P(pair, grp), P()),
        out_specs=P(pair, None, grp),
        check_vma=False,
    )
```

```python
import jax
import jax.numpy as jnp
import numpy as np
from jax import lax
from jax.experimental import pallas as pl
from jax.experimental.pallas import tpu as pltpu
from jax.sharding import Mesh
from jax.sharding import PartitionSpec as P

VB = 96
OCC = 3
GRPS = 8
PAIRS = 32
ZS = 8
SLAB = VB // GRPS
PIECE = SLAB // 4 * SLAB
LANES = 384
CHUNK = 1152
WIRE = jnp.float16
SCALE = 16.0
BF, F32 = jnp.bfloat16, jnp.float32
ORDER = ("y", "xh", "xl", "c", "z")
SWAP = [(0, 1), (1, 0)]


def mm(x, y):
    return jnp.dot(x, y, preferred_element_type=F32)


def halves(x):
    hi = x.astype(BF)
    return hi, (x - hi.astype(F32)).astype(BF)


def selector(size, source):
    rows = np.arange(size)
    chosen = np.zeros((size, size), np.float32)
    chosen[rows, source(rows)] = 1
    return jnp.asarray(chosen, BF)


def folded(block):
    tall, third = block.shape[0] // 4, block.shape[1] // 3
    rest = [block[3 * tall :, n * third : (n + 1) * third] for n in range(3)]
    return jnp.concatenate([block[: 3 * tall], jnp.concatenate(rest, axis=0)], axis=1)


def product_kernel(place_ref, *refs):
    t_refs, pieces, refs = refs[:6], refs[6 : 6 + 2 * ZS], refs[6 + 2 * ZS :]
    row_ref, col_ref, near_ref, far_ref, out_ref, acc_ref, turned_ref, stage_ref, w_ref, sem = refs
    step = pl.program_id(0)

    @pl.when(step == 0)
    def _():
        acc_ref[...] = jnp.zeros_like(acc_ref)
        copies = [
            pltpu.make_async_copy(piece, stage_ref.at[n], sem.at[n])
            for n, piece in enumerate(pieces)
        ]
        for copy in copies:
            copy.start()
        for copy in copies:
            copy.wait()
        z, xl, c = place_ref[0], place_ref[1], place_ref[2]
        tall, width = stage_ref.shape[1] // 3, w_ref.shape[1]
        for n in range(2 * ZS):
            k = n % ZS
            back = jnp.where(c == 0, k, ZS - k)
            of = jnp.where(n < ZS, xl, 1 - xl) * ZS + lax.rem(z + ZS - back, ZS)
            start = pl.multiple_of(of * (4 * tall), 4 * tall)
            w_ref[pl.ds(start, 3 * tall)] = stage_ref[n, :, :width]
            rest = [stage_ref[n, m * tall : (m + 1) * tall, width:] for m in range(3)]
            w_ref[pl.ds(start + 3 * tall, tall)] = jnp.concatenate(rest, axis=1)

    size = row_ref.shape[0]
    w = w_ref[pl.ds(pl.multiple_of(step * CHUNK, CHUNK), CHUNK)]

    def add(*t_refs):
        t = jnp.concatenate([t_ref[...] for t_ref in t_refs], axis=0)
        acc_ref[...] += lax.dot_general(w, t, (((0,), (1,)), ((), ())), preferred_element_type=F32)

    early = step < pl.num_programs(0) // 2

    @pl.when(early)
    def _():
        add(*t_refs[:4])

    @pl.when(jnp.logical_not(early))
    def _():
        add(*t_refs[:2], *t_refs[4:])

    @pl.when(step == pl.num_programs(0) - 1)
    def _():
        ladder = acc_ref[...].T
        near_ref[...], far_ref[...] = ladder[: 2 * size], ladder[2 * size :]
        for o in range(4):
            total = 0.0
            for part in halves(ladder[o * size : (o + 1) * size] * SCALE):
                total += mm(mm(row_ref[...], part).astype(BF), col_ref[...])
            turned_ref[o] = total
        fill = jnp.zeros((PAIRS, LANES - OCC * OCC * PIECE), F32)
        for g in range(GRPS):
            planes = []
            for o in range(4):
                cut = [
                    turned_ref[o, q * PAIRS : (q + 1) * PAIRS, g * PIECE : (g + 1) * PIECE]
                    for q in range(OCC * OCC)
                ]
                planes.append(jnp.concatenate([*cut, fill], axis=1))
            message = jnp.swapaxes(jnp.stack(planes, axis=0), 0, 1)
            out_ref[g * PAIRS : (g + 1) * PAIRS] = message


def unpack_kernel(
    place_ref, live_ref, got_ref, own_ref, side_ref, far_ref, row_ref, col_ref, out_ref, v_ref
):
    for g in range(GRPS):
        v_ref[g] = jnp.swapaxes(got_ref[g * PAIRS : (g + 1) * PAIRS], 0, 1)
    blocks = []
    for j in range(OCC):
        for xl in range(2):
            for c in range(2):
                for i in range(OCC):
                    at = (i * OCC + j) * PIECE
                    cut = []
                    for g in range(GRPS):
                        for xs in range(2):
                            for cs in range(2):
                                z = (xs * 2 + cs) * ZS
                                o = (xl ^ xs) * 2 + (c ^ cs)
                                cut.append(v_ref[g, o, z : z + ZS, at : at + PIECE])
                    blocks.append(jnp.concatenate(cut, axis=1))
    stacked = jnp.concatenate(blocks, axis=0)
    total = 0.0
    for part in halves(stacked):
        total += mm(mm(row_ref[...], part).astype(BF), col_ref[...])

    def joined(first, x, y):
        return jnp.where(
            first, jnp.concatenate([x, y], axis=1), jnp.concatenate([y, x], axis=1)
        )

    near = joined(place_ref[1] == 0, own_ref[...], side_ref[0])
    far = joined(place_ref[1] == 0, far_ref[...], side_ref[1])
    summed = joined(place_ref[2] == 0, near, far) + total * (1 / SCALE)
    col = lax.broadcasted_iota(jnp.int32, summed.shape, 1)
    first = place_ref[0] * SLAB + col // VB
    keep = (first < live_ref[0]) & (col % VB < live_ref[0])
    out_ref[...] = jnp.where(keep, summed, 0.0).astype(BF)


def around(x, axes, size):
    moves = [(i * 2, (i + 1) % size * 2) for i in range(size)]
    moves += [(i * 2 + 1, (i - 1) % size * 2 + 1) for i in range(size)]
    return lax.ppermute(x, (*axes, "c"), moves)


def ring(block):
    blocks = [block]
    for _ in range(ZS - 1):
        blocks.append(around(blocks[-1], ("z",), ZS))
    return blocks


def on_device(amplitudes, integrals, live_counts):
    occ, nocc, k_all = amplitudes.shape
    shard, slab = integrals.shape
    rows, quarter = occ * nocc, slab // 4
    xl, z, c = lax.axis_index("xl"), lax.axis_index("z"), lax.axis_index("c")
    grp = lax.axis_index("y") * 2 + lax.axis_index("xh")

    cols = [integrals[:, n * quarter : (n + 1) * quarter] for n in range(4)]
    first = c == 0
    w_keep = jnp.concatenate(
        [jnp.where(first, cols[0], cols[1]), jnp.where(first, cols[2], cols[3])], axis=0
    )
    w_send = jnp.concatenate(
        [jnp.where(first, cols[1], cols[0]), jnp.where(first, cols[3], cols[2])], axis=0
    )
    w_side = lax.ppermute(w_send, "c", SWAP)
    at = (xl * ZS + z) * 2 * shard + jnp.arange(2 * shard)
    live = ((at // VB < live_counts[1]) & (at % VB < live_counts[1]))[:, None]
    both = []
    for n in range(2):
        keep, side = w_keep[n * shard : (n + 1) * shard], w_side[n * shard : (n + 1) * shard]
        stacked = jnp.where(
            first,
            jnp.concatenate([keep, side], axis=0),
            jnp.concatenate([side, keep], axis=0),
        )
        both.append(jnp.where(live, stacked, 0))
    near = jnp.where(xl == 0, both[0], both[1])
    far = lax.ppermute(folded(jnp.where(xl == 0, both[1], both[0])), "xl", SWAP)
    ring_near, ring_far = ring(folded(near)), ring(far)
    pieces = ring_near + ring_far

    t = amplitudes.reshape(rows, k_all)
    t_a, t_b, _ = lax.optimization_barrier(
        (t[:, : k_all // 2], t[:, k_all // 2 :], (far, ring_near[1]))
    )
    x_a, x_b = around(t_a, ("xh", "xl"), 4), around(t_b, ("xh", "xl"), 4)
    x_a, *_ = lax.optimization_barrier((x_a, ring_near[5], ring_far[4]))
    x_b, *_ = lax.optimization_barrier((x_b, ring_near[-1], ring_far[-1]))
    t_c, c_a, c_b = (lax.ppermute(x, "c", SWAP) for x in (t, x_a, x_b))
    t_refs = [t, t_c, x_a, c_a, x_b, c_b]

    out_cols = selector(quarter, lambda r: ((r // SLAB) % GRPS) * PIECE + r // VB * SLAB + r % SLAB)
    in_cols = selector(slab, lambda r: (r % SLAB) * VB + r // SLAB)
    out_rows = selector(
        rows,
        lambda r: r // nocc * nocc
        + (r % PAIRS // 16) * 48
        + (r % ZS) * 6
        + (r // ZS % 2) * 3
        + r // PAIRS % OCC,
    )
    in_rows = selector(rows, lambda r: r // 48 * 48 + (r // 3 % 2) * 24 + (r % 3) * 8 + r // 6 % ZS)

    params = pltpu.CompilerParams(vmem_limit_bytes=34 * 2**20)
    half = k_all // CHUNK // 2
    fixed = lambda k: (0, 0)
    full = lambda k: (0, k)
    early = lambda k: (0, jnp.minimum(k, half - 1))
    late = lambda k: (0, jnp.maximum(k - half, 0))
    p_near, p_far, wire = pl.pallas_call(
        product_kernel,
        grid=(k_all // CHUNK,),
        in_specs=[pl.BlockSpec(memory_space=pltpu.SMEM)]
        + [pl.BlockSpec((rows, CHUNK), chunk) for chunk in (full, full, early, early, late, late)]
        + [pl.BlockSpec(memory_space=pl.ANY)] * len(pieces)
        + [
            pl.BlockSpec((rows, rows), fixed),
            pl.BlockSpec((quarter, quarter), fixed),
        ],
        out_specs=[
            pl.BlockSpec((2 * rows, quarter), fixed),
            pl.BlockSpec((2 * rows, quarter), fixed),
            pl.BlockSpec((GRPS * PAIRS, 4, LANES), lambda k: (0, 0, 0)),
        ],
        out_shape=[
            jax.ShapeDtypeStruct((2 * rows, quarter), F32),
            jax.ShapeDtypeStruct((2 * rows, quarter), F32),
            jax.ShapeDtypeStruct((GRPS * PAIRS, 4, LANES), F32),
        ],
        scratch_shapes=[
            pltpu.VMEM((quarter, 4 * rows), F32),
            pltpu.VMEM((4, rows, quarter), F32),
            pltpu.VMEM((2 * ZS, *far.shape), BF),
            pltpu.VMEM((k_all, quarter), BF),
            pltpu.SemaphoreType.DMA((len(pieces),)),
        ],
        compiler_params=params,
    )(jnp.stack([z, xl, c]), *t_refs, *pieces, out_rows, out_cols)

    fetched = lax.ppermute(p_far, "xl", SWAP)
    side = lax.ppermute(jnp.stack([p_near[rows:], fetched[rows:]]), "c", SWAP)

    got = lax.all_to_all(wire.astype(WIRE), ORDER, 0, 0, tiled=True)
    whole = pl.BlockSpec(memory_space=pltpu.VMEM)
    small = pl.BlockSpec(memory_space=pltpu.SMEM)
    out = pl.pallas_call(
        unpack_kernel,
        out_shape=jax.ShapeDtypeStruct((rows, slab), BF),
        in_specs=[small, small] + [whole] * 6,
        scratch_shapes=[pltpu.VMEM((GRPS, 4, PAIRS, LANES), F32)],
        compiler_params=params,
    )(
        jnp.stack([grp, c, xl]),
        live_counts,
        got.astype(F32),
        p_near[:rows],
        side,
        fetched[:rows],
        in_rows,
        in_cols,
    )
    return out.reshape(occ, nocc, slab)


def solution(mesh):
    fine = Mesh(mesh.devices.reshape(4, 2, 2, 8, 2), ("y", "xh", "xl", "z", "c"))
    pair, grp = ("xl", "z", "c"), ("y", "xh")
    return jax.shard_map(
        on_device,
        mesh=fine,
        in_specs=(P(pair, None, None), P(pair, grp), P()),
        out_specs=P(pair, None, grp),
        check_vma=False,
    )
```

```python
import jax
import jax.numpy as jnp
import numpy as np
from jax import lax
from jax.experimental import pallas as pl
from jax.experimental.pallas import tpu as pltpu
from jax.sharding import Mesh
from jax.sharding import PartitionSpec as P

VB = 96
OCC = 3
GRPS = 8
PAIRS = 32
ZS = 8
SLAB = VB // GRPS
PIECE = SLAB // 4 * SLAB
LANES = 384
TILE = 128
CHUNK = 1536
WIRE = jnp.float16
SCALE = 16.0
BF, F32 = jnp.bfloat16, jnp.float32
ORDER = ("y", "xh", "xl", "c", "z")
SWAP = [(0, 1), (1, 0)]


def mm(x, y):
    return jnp.dot(x, y, preferred_element_type=F32)


def halves(x):
    hi = x.astype(BF)
    return hi, (x - hi.astype(F32)).astype(BF)


def selector(size, source):
    rows = np.arange(size)
    chosen = np.zeros((size, size), np.float32)
    chosen[rows, source(rows)] = 1
    return jnp.asarray(chosen, BF)


def folded(block):
    tall, full = block.shape[0] // 4, block.shape[1] // TILE * TILE
    rest = [block[n * tall : (n + 1) * tall, full:] for n in range(4)]
    tiles = [block[:, n : n + TILE] for n in range(0, full, TILE)]
    return jnp.concatenate([*tiles, jnp.concatenate(rest, axis=1)], axis=0)


def product_kernel(place_ref, *refs):
    t_refs, pieces, refs = refs[:6], refs[6 : 6 + 2 * ZS], refs[6 + 2 * ZS :]
    row_ref, col_ref, near_ref, far_ref, out_ref, acc_ref, turned_ref, stage_ref, w_ref, sem = refs
    step = pl.program_id(0)

    @pl.when(step == 0)
    def _():
        acc_ref[...] = jnp.zeros_like(acc_ref)
        z, xl, c = place_ref[0], place_ref[1], place_ref[2]
        tall, width = stage_ref.shape[1], w_ref.shape[1]
        tiles = width // TILE
        starts, copies = [], []
        for n, piece in enumerate(pieces):
            k = n % ZS
            back = jnp.where(c == 0, k, ZS - k)
            of = jnp.where(n < ZS, xl, 1 - xl) * ZS + lax.rem(z + ZS - back, ZS)
            start = pl.multiple_of(of * (4 * tall), 4 * tall)
            starts.append(start)
            for m in range(tiles):
                copies.append(
                    pltpu.make_async_copy(
                        piece.at[pl.ds(m * 4 * tall, 4 * tall)],
                        w_ref.at[pl.ds(start, 4 * tall), pl.ds(m * TILE, TILE)],
                        sem.at[n, m],
                    )
                )
            copies.append(
                pltpu.make_async_copy(
                    piece.at[pl.ds(tiles * 4 * tall, tall)], stage_ref.at[n], sem.at[n, tiles]
                )
            )
        for copy in copies:
            copy.start()
        for copy in copies:
            copy.wait()
        wide = width - tiles * TILE
        for n, start in enumerate(starts):
            for m in range(4):
                w_ref[pl.ds(start + m * tall, tall), tiles * TILE :] = stage_ref[
                    n, :, m * wide : (m + 1) * wide
                ]

    size = row_ref.shape[0]
    w = w_ref[pl.ds(pl.multiple_of(step * CHUNK, CHUNK), CHUNK)]

    def add(*t_refs):
        t = jnp.concatenate([t_ref[...] for t_ref in t_refs], axis=0)
        acc_ref[...] += lax.dot_general(w, t, (((0,), (1,)), ((), ())), preferred_element_type=F32)

    early = step < pl.num_programs(0) // 2

    @pl.when(early)
    def _():
        add(*t_refs[:4])

    @pl.when(jnp.logical_not(early))
    def _():
        add(*t_refs[:2], *t_refs[4:])

    @pl.when(step == pl.num_programs(0) - 1)
    def _():
        ladder = acc_ref[...].T
        near_ref[...], far_ref[...] = ladder[: 2 * size], ladder[2 * size :]
        for o in range(4):
            total = 0.0
            for part in halves(ladder[o * size : (o + 1) * size] * SCALE):
                total += mm(mm(row_ref[...], part).astype(BF), col_ref[...])
            turned_ref[o] = total
        fill = jnp.zeros((PAIRS, LANES - OCC * OCC * PIECE), F32)
        for g in range(GRPS):
            planes = []
            for o in range(4):
                cut = [
                    turned_ref[o, q * PAIRS : (q + 1) * PAIRS, g * PIECE : (g + 1) * PIECE]
                    for q in range(OCC * OCC)
                ]
                planes.append(jnp.concatenate([*cut, fill], axis=1))
            message = jnp.swapaxes(jnp.stack(planes, axis=0), 0, 1)
            out_ref[g * PAIRS : (g + 1) * PAIRS] = message


def unpack_kernel(
    place_ref, live_ref, got_ref, own_ref, side_ref, far_ref, row_ref, col_ref, out_ref, v_ref
):
    for g in range(GRPS):
        v_ref[g] = jnp.swapaxes(got_ref[g * PAIRS : (g + 1) * PAIRS], 0, 1)
    blocks = []
    for j in range(OCC):
        for xl in range(2):
            for c in range(2):
                for i in range(OCC):
                    at = (i * OCC + j) * PIECE
                    cut = []
                    for g in range(GRPS):
                        for xs in range(2):
                            for cs in range(2):
                                z = (xs * 2 + cs) * ZS
                                o = (xl ^ xs) * 2 + (c ^ cs)
                                cut.append(v_ref[g, o, z : z + ZS, at : at + PIECE])
                    blocks.append(jnp.concatenate(cut, axis=1))
    stacked = jnp.concatenate(blocks, axis=0)
    total = 0.0
    for part in halves(stacked):
        total += mm(mm(row_ref[...], part).astype(BF), col_ref[...])

    def joined(first, x, y):
        return jnp.where(
            first, jnp.concatenate([x, y], axis=1), jnp.concatenate([y, x], axis=1)
        )

    near = joined(place_ref[1] == 0, own_ref[...], side_ref[0])
    far = joined(place_ref[1] == 0, far_ref[...], side_ref[1])
    summed = joined(place_ref[2] == 0, near, far) + total * (1 / SCALE)
    col = lax.broadcasted_iota(jnp.int32, summed.shape, 1)
    first = place_ref[0] * SLAB + col // VB
    keep = (first < live_ref[0]) & (col % VB < live_ref[0])
    out_ref[...] = jnp.where(keep, summed, 0.0).astype(BF)


def around(x, axes, size):
    moves = [(i * 2, (i + 1) % size * 2) for i in range(size)]
    moves += [(i * 2 + 1, (i - 1) % size * 2 + 1) for i in range(size)]
    return lax.ppermute(x, (*axes, "c"), moves)


def ring(block):
    blocks = [block]
    for _ in range(ZS - 1):
        blocks.append(around(blocks[-1], ("z",), ZS))
    return blocks


def on_device(amplitudes, integrals, live_counts):
    occ, nocc, k_all = amplitudes.shape
    shard, slab = integrals.shape
    rows, quarter = occ * nocc, slab // 4
    xl, z, c = lax.axis_index("xl"), lax.axis_index("z"), lax.axis_index("c")
    grp = lax.axis_index("y") * 2 + lax.axis_index("xh")

    cols = [integrals[:, n * quarter : (n + 1) * quarter] for n in range(4)]
    first = c == 0
    w_keep = jnp.concatenate(
        [jnp.where(first, cols[0], cols[1]), jnp.where(first, cols[2], cols[3])], axis=0
    )
    w_send = jnp.concatenate(
        [jnp.where(first, cols[1], cols[0]), jnp.where(first, cols[3], cols[2])], axis=0
    )
    w_side = lax.ppermute(w_send, "c", SWAP)
    at = (xl * ZS + z) * 2 * shard + jnp.arange(2 * shard)
    live = ((at // VB < live_counts[1]) & (at % VB < live_counts[1]))[:, None]
    both = []
    for n in range(2):
        keep, side = w_keep[n * shard : (n + 1) * shard], w_side[n * shard : (n + 1) * shard]
        stacked = jnp.where(
            first,
            jnp.concatenate([keep, side], axis=0),
            jnp.concatenate([side, keep], axis=0),
        )
        both.append(jnp.where(live, stacked, 0))
    near = jnp.where(xl == 0, both[0], both[1])
    far = lax.ppermute(folded(jnp.where(xl == 0, both[1], both[0])), "xl", SWAP)
    ring_near, ring_far = ring(folded(near)), ring(far)
    pieces = ring_near + ring_far

    t = amplitudes.reshape(rows, k_all)
    t_a, t_b, _ = lax.optimization_barrier(
        (t[:, : k_all // 2], t[:, k_all // 2 :], (far, ring_near[1]))
    )
    x_a, x_b = around(t_a, ("xh", "xl"), 4), around(t_b, ("xh", "xl"), 4)
    x_a, *_ = lax.optimization_barrier((x_a, ring_near[5], ring_far[4]))
    x_b, *_ = lax.optimization_barrier((x_b, ring_near[-1], ring_far[-1]))
    t_c, c_a, c_b = (lax.ppermute(x, "c", SWAP) for x in (t, x_a, x_b))
    t_refs = [t, t_c, x_a, c_a, x_b, c_b]

    out_cols = selector(quarter, lambda r: ((r // SLAB) % GRPS) * PIECE + r // VB * SLAB + r % SLAB)
    in_cols = selector(slab, lambda r: (r % SLAB) * VB + r // SLAB)
    out_rows = selector(
        rows,
        lambda r: r // nocc * nocc
        + (r % PAIRS // 16) * 48
        + (r % ZS) * 6
        + (r // ZS % 2) * 3
        + r // PAIRS % OCC,
    )
    in_rows = selector(rows, lambda r: r // 48 * 48 + (r // 3 % 2) * 24 + (r % 3) * 8 + r // 6 % ZS)

    params = pltpu.CompilerParams(vmem_limit_bytes=34 * 2**20)
    half = k_all // CHUNK // 2
    fixed = lambda k: (0, 0)
    full = lambda k: (0, k)
    early = lambda k: (0, jnp.minimum(k, half - 1))
    late = lambda k: (0, jnp.maximum(k - half, 0))
    p_near, p_far, wire = pl.pallas_call(
        product_kernel,
        grid=(k_all // CHUNK,),
        in_specs=[pl.BlockSpec(memory_space=pltpu.SMEM)]
        + [pl.BlockSpec((rows, CHUNK), chunk) for chunk in (full, full, early, early, late, late)]
        + [pl.BlockSpec(memory_space=pl.ANY)] * len(pieces)
        + [
            pl.BlockSpec((rows, rows), fixed),
            pl.BlockSpec((quarter, quarter), fixed),
        ],
        out_specs=[
            pl.BlockSpec((2 * rows, quarter), fixed),
            pl.BlockSpec((2 * rows, quarter), fixed),
            pl.BlockSpec((GRPS * PAIRS, 4, LANES), lambda k: (0, 0, 0)),
        ],
        out_shape=[
            jax.ShapeDtypeStruct((2 * rows, quarter), F32),
            jax.ShapeDtypeStruct((2 * rows, quarter), F32),
            jax.ShapeDtypeStruct((GRPS * PAIRS, 4, LANES), F32),
        ],
        scratch_shapes=[
            pltpu.VMEM((quarter, 4 * rows), F32),
            pltpu.VMEM((4, rows, quarter), F32),
            pltpu.VMEM((2 * ZS, shard // 2, TILE), BF),
            pltpu.VMEM((k_all, quarter), BF),
            pltpu.SemaphoreType.DMA((len(pieces), quarter // TILE + 1)),
        ],
        compiler_params=params,
    )(jnp.stack([z, xl, c]), *t_refs, *pieces, out_rows, out_cols)

    fetched = lax.ppermute(p_far, "xl", SWAP)
    side = lax.ppermute(jnp.stack([p_near[rows:], fetched[rows:]]), "c", SWAP)

    got = lax.all_to_all(wire.astype(WIRE), ORDER, 0, 0, tiled=True)
    whole = pl.BlockSpec(memory_space=pltpu.VMEM)
    small = pl.BlockSpec(memory_space=pltpu.SMEM)
    out = pl.pallas_call(
        unpack_kernel,
        out_shape=jax.ShapeDtypeStruct((rows, slab), BF),
        in_specs=[small, small] + [whole] * 6,
        scratch_shapes=[pltpu.VMEM((GRPS, 4, PAIRS, LANES), F32)],
        compiler_params=params,
    )(
        jnp.stack([grp, c, xl]),
        live_counts,
        got.astype(F32),
        p_near[:rows],
        side,
        fetched[:rows],
        in_rows,
        in_cols,
    )
    return out.reshape(occ, nocc, slab)


def solution(mesh):
    fine = Mesh(mesh.devices.reshape(4, 2, 2, 8, 2), ("y", "xh", "xl", "z", "c"))
    pair, grp = ("xl", "z", "c"), ("y", "xh")
    return jax.shard_map(
        on_device,
        mesh=fine,
        in_specs=(P(pair, None, None), P(pair, grp), P()),
        out_specs=P(pair, None, grp),
        check_vma=False,
    )
```
